128 devices in a mesh: subset: 8 (over z, y_hi), tile: 16 (over x, y_lo, core).
Axes of the slice: x: 4, y: 4 (y_hi: 2, y_lo: 2; y = y_hi * 2 + y_lo), z: 4, core: 2. Of those that a mesh axis runs over, the one named last changes fastest.
Arguments:
- start_volume: float32 [16384, 2048], P('tile', 'subset'), may hold values from 0 to 2
- tiles: bfloat16 [8, 128, 8, 128, 128], P('subset', 'tile'), may hold values from 5e-05 to 30
- pattern: int32 [8, 128, 8], P('subset', 'tile'), may hold values from 0 to 15, as said below
- projections: float32 [8, 2048, 2048], P('subset', 'tile'), may hold values from 0.5 to 1.5
Outputs:
- volume: float32 [16384, 2048], P('tile', 'subset')
The draws below stay inside these ranges and needn't reach their ends.
Inputs may be any that keep to these rules, and one draw needn't show every extreme that they name: `pattern`: for each subset and pixel block the 8 ray blocks differ; in each subset every ray block is named by some pixel block.
All inputs are finite; a program needn't handle non-finite values.
Results may differ from the reference program's by a relative error of at most 0.00031.
Values may be sent and summed in bfloat16 or wider, within the bound.
A program may use at most 64 MiB of HBM per device.

```python
import math
import jax
import jax.numpy as jnp

BLK = 128
NNZ = 8
GSL = 128
GRP_DEV = 2
ITERS = 1
SUBSETS = 8
RAYB = 16
RAYS = 2048
PBT = 128
PIX = 16384
SLICES = 2048
N_SUBSET = 8
N_TILE = 16


def draw_pattern(key, part):
    key = jax.random.fold_in(key, 7)
    scores = jax.random.randint(key, (SUBSETS, PBT, RAYB), 0, 4096)
    column = jnp.arange(RAYB, dtype=jnp.int32)[None, None, :]
    row = jnp.arange(PBT, dtype=jnp.int32)[None, :, None]
    forced = column == row % RAYB
    ranked = jnp.where(forced, -1, scores) * RAYB + column
    order = jnp.argsort(ranked, axis=-1, stable=True).astype(jnp.int32)
    return order[:, :, :NNZ]


def draw_tiles(key, part):
    key = jax.random.fold_in(key, 11)
    keys = jax.random.split(key, 5)
    factor_lo, factor_hi, scale_lo, scale_hi, floor_lo, floor_hi = (0.5, 1.5, 0.3, 3.0, 0.5, 1.5)
    shape = (SUBSETS, PBT, NNZ, BLK, BLK)
    offset = jax.random.randint(keys[0], (SUBSETS, PBT, NNZ, 1, 1), 0, BLK)
    ray_index = jnp.arange(BLK, dtype=jnp.int32)[:, None]
    pixel_index = jnp.arange(BLK, dtype=jnp.int32)[None, :]
    distance = jnp.mod(pixel_index - ray_index - offset, BLK)
    distance = jnp.minimum(distance, BLK - distance).astype(jnp.float32) / 1.5
    band = jnp.exp(-0.5 * distance * distance)
    factor = jax.random.uniform(keys[1], shape, jnp.float32, factor_lo, factor_hi)
    floor_part = jax.random.uniform(keys[2], shape, jnp.float32, floor_lo, floor_hi)
    row_scale = jnp.exp(jax.random.uniform(keys[3], (SUBSETS, PBT, NNZ, BLK, 1), jnp.float32, math.log(scale_lo), math.log(scale_hi)))
    col_scale = jnp.exp(jax.random.uniform(keys[4], (SUBSETS, PBT, 1, 1, BLK), jnp.float32, math.log(scale_lo), math.log(scale_hi)))
    return (row_scale * col_scale * (factor * band + 0.01 * floor_part)).astype(jnp.bfloat16)


def shard_levels(own_key, dims, cuts, low, largest):
    def one(axis_at, blocks):
        draws = jax.random.uniform(jax.random.fold_in(jax.random.fold_in(own_key, 6), axis_at), (blocks,), jnp.float32, low / len(cuts), largest / len(cuts))
        return jnp.repeat(jnp.exp(draws), dims[axis_at] // blocks).reshape((-1,) + (1,) * (len(dims) - axis_at - 1))

    gain = one(*cuts[0])
    for cut in cuts[1:]:
        gain = gain * one(*cut)
    return gain


def setup_inputs(seed: int = 0) -> dict:
    key_of = jax.random.split(jax.random.key(seed), 5)
    start_volume = jnp.clip(2.0 * jax.random.uniform(key_of[0], (PIX, SLICES), jnp.float32) ** shard_levels(key_of[0], (PIX, SLICES), ((0, 16), (1, 8)), -0.2, 0.2), 0.0, 2.0)
    tiles = draw_tiles(jax.random.fold_in(key_of[4], 71), 0)
    pattern = draw_pattern(jax.random.fold_in(key_of[4], 71), 0)
    projections = jnp.clip(0.5 + 1.0 * jax.random.uniform(key_of[3], (SUBSETS, RAYS, SLICES), jnp.float32) ** shard_levels(key_of[3], (SUBSETS, RAYS, SLICES), ((0, 8), (1, 16)), -0.2, 0.2), 0.5, 1.5)
    return dict(start_volume=start_volume, tiles=tiles, pattern=pattern, projections=projections)


def reference(start_volume, tiles, pattern, projections):
    columns = GRP_DEV * GSL
    weights_rows = []
    weights_cols = []
    for subset_id in range(N_SUBSET):
        tile_set = tiles[subset_id].astype(jnp.float32)
        links = pattern[subset_id].reshape(-1).astype(jnp.int32)
        row_sum = jnp.sum(tile_set, axis=-1).reshape(-1, BLK)
        weights_rows.append(jnp.zeros((N_TILE, BLK), jnp.float32).at[links].add(row_sum))
        weights_cols.append(jnp.sum(tile_set, axis=(1, 2)).reshape(-1, 1))
    blocks_out = []
    for block_id in range(N_SUBSET):
        panel = start_volume[:, block_id * columns:(block_id + 1) * columns]
        for step in range(ITERS * N_SUBSET):
            subset_id = (block_id + step) % N_SUBSET
            tile_set = tiles[subset_id].astype(jnp.float32)
            links = pattern[subset_id].astype(jnp.int32)
            image = panel.astype(jnp.bfloat16).astype(jnp.float32).reshape(-1, BLK, columns)
            contrib = jnp.einsum('qkrp,qps->qkrs', tile_set, image)
            ray_sums = jnp.zeros((N_TILE, BLK, columns), jnp.float32).at[links.reshape(-1)].add(contrib.reshape(-1, BLK, columns))
            measured = projections[subset_id][:, block_id * columns:(block_id + 1) * columns].reshape(N_TILE, BLK, columns)
            residual = (measured - ray_sums / weights_rows[subset_id][:, :, None]).astype(jnp.bfloat16)
            chosen = residual[links].astype(jnp.float32)
            correction = jnp.einsum('qkrp,qkrs->qps', tile_set, chosen).reshape(-1, columns)
            panel = panel + 0.9 * correction / weights_cols[subset_id]
        blocks_out.append(panel)
    return jnp.concatenate(blocks_out, axis=1)
```

```python
import jax
import jax.numpy as jnp
from jax import lax
from jax.experimental import pallas as pl
from jax.experimental.pallas import tpu as pltpu
from jax.sharding import PartitionSpec as P

MESH = pl.DeviceIdType.MESH
BLK = 128
STEPS = 8
CHIPS = 8
COLS = 256
PAD = 16
ROWS = COLS + PAD
PIXELS = 1024
RAYS = 2048
CHUNKS = ((0, 144), (144, 128))


def split3(w):
    row = lax.broadcasted_iota(jnp.int32, w.shape, 0)
    hi = w.astype(jnp.bfloat16).astype(jnp.float32)
    rest = w - hi
    mid = rest.astype(jnp.bfloat16).astype(jnp.float32)
    low = rest - mid
    out = jnp.where(row == 0, hi, jnp.where(row == 1, mid, jnp.where(row == 2, low, 0.0)))
    return out.astype(jnp.bfloat16)


def kernel(
    vol_ref, tile_ref, inv_ref, inv0_ref, proj_ref, out_ref,
    tb, inv_v, inv_s, pm, dense, xe, mine, c1s, c1r, rss, rs, loc, wtot, re,
    tile_sem, inv_send, inv_recv, inv_copy, pm_send, pm_recv, t_send, t_recv,
    c1_send, c1_recv, rs_send, rs_recv, ag_send, ag_recv, c2_send, c2_recv,
):
    c = lax.axis_index("subset")
    t = lax.axis_index("tile")
    z, h = c // 2, c % 2
    x, l, k = t // 4, (t // 2) % 2, t % 2

    def chip(mr):
        return (c, (((x + mr // 2) % 4) * 2 + (l + mr % 2) % 2) * 2 + k)

    def back(mr):
        return ((4 - mr // 2) % 4) * 2 + mr % 2

    core = (c, t + 1 - 2 * k)

    def group(d):
        return ((c + d) % STEPS, t)

    z_dev = {-1: (((z + 3) % 4) * 2 + h, t), 1: (((z + 1) % 4) * 2 + h, t)}
    y_dev = (z * 2 + 1 - h, t)

    own = pltpu.make_async_copy(tile_ref, tb[0], tile_sem)
    own.start()

    barrier = pltpu.get_barrier_semaphore()
    for mr in range(1, CHIPS):
        pl.semaphore_signal(barrier, inc=1, device_id=chip(mr), device_id_type=MESH)
    pl.semaphore_signal(barrier, inc=1, device_id=core, device_id_type=MESH)
    for d in range(1, STEPS):
        pl.semaphore_signal(barrier, inc=1, device_id=group(d), device_id_type=MESH)
    pl.semaphore_wait(barrier, CHIPS - 1 + 1 + STEPS - 1)
    own.wait()

    def piece(slot, p):
        return tb[slot].at[pl.ds(4 * p, 4)]

    def tile_copy(idx, src, p, dst, device):
        return pltpu.make_async_remote_copy(
            src_ref=piece(src, p), dst_ref=piece(dst, p), send_sem=t_send.at[idx],
            recv_sem=t_recv.at[dst, p], device_id=device, device_id_type=MESH,
        )

    flows = (
        {
            0: [("-", 0, 0, 2), ("+", 0, 0, 6), ("y", 0, 1, 7)],
            1: [("-", 1, 1, 3), ("+", 6, 0, 4), ("y", 2, 0, 1)],
            2: [("-", 0, 1, 2), ("+", 0, 1, 6), ("y", 4, 0, 3)],
            3: [("-", 3, 1, 5), ("+", 1, 1, 7), ("y", 6, 0, 5)],
            4: [("-", 2, 1, 4), ("y", 0, 0, 7)],
        },
        {
            0: [("-", 0, 0, 2), ("+", 0, 0, 6), ("y", 0, 1, 1)],
            1: [("-", 7, 1, 1), ("+", 6, 0, 4), ("y", 0, 0, 1)],
            2: [("-", 0, 1, 2), ("+", 0, 1, 6), ("y", 2, 0, 3)],
            3: [("-", 1, 1, 3), ("+", 7, 1, 5), ("y", 4, 0, 5)],
            4: [("-", 2, 1, 4), ("y", 6, 0, 7)],
        },
    )
    waited = (set(), set())

    def need(row, slot, p):
        if slot and (slot, p) not in waited[row]:
            waited[row].add((slot, p))
            pltpu.make_async_remote_copy(
                src_ref=piece(slot, p), dst_ref=piece(slot, p), send_sem=t_send.at[0],
                recv_sem=t_recv.at[slot, p], device_id=y_dev, device_id_type=MESH,
            ).wait_recv()

    def flow_copies(row, point):
        for i, (way, src, p, dst) in enumerate(flows[row][point]):
            device = y_dev if way == "y" else z_dev[-1 if way == "-" else 1]
            yield src, p, tile_copy(3 * point + i, src, p, dst, device)

    def tile_point(point):
        for row in range(2):
            @pl.when(h == row)
            def _():
                for src, p, copy in flow_copies(row, point):
                    need(row, src, p)
                    copy.start()

    def tile_drain():
        for row in range(2):
            @pl.when(h == row)
            def _():
                for point in range(5):
                    for _, _, copy in flow_copies(row, point):
                        copy.wait_send()

    def tile_wait(slot):
        for row in range(2):
            @pl.when(h == row)
            def _():
                need(row, slot, 0)
                need(row, slot, 1)

    def pm_copy(slot):
        d = STEPS - slot
        return pltpu.make_async_remote_copy(
            src_ref=proj_ref.at[pl.ds(pl.multiple_of(((c + d) % STEPS) * COLS, COLS), COLS)],
            dst_ref=pm.at[slot], send_sem=pm_send.at[slot], recv_sem=pm_recv.at[slot],
            device_id=group(d), device_id_type=MESH,
        )

    def inv_copy_to(slot):
        return pltpu.make_async_remote_copy(
            src_ref=inv_ref, dst_ref=inv_v.at[slot], send_sem=inv_send.at[slot],
            recv_sem=inv_recv.at[slot], device_id=group(STEPS - slot), device_id_type=MESH,
        )

    for slot in range(1, STEPS):
        inv_copy_to(slot).start()
    pm_copy(1).start()
    tile_point(0)

    def assemble(slot):
        dn = dense.at[slot % 2]
        if slot:
            inv_copy_to(slot).wait_recv()
            local = pltpu.make_async_copy(inv_v.at[slot], inv_s.at[slot], inv_copy)
            local.start()
            local.wait()
            tile_wait(slot)

        def block(i, _):
            mr, j = i // 2, i % 2
            b = (((x + mr // 2) % 4) * 2 + (l + mr % 2) % 2) * 2 + (k + j) % 2
            for q in range(8):
                at = inv_s[slot, q, b] if slot else inv0_ref[q, b]
                tile = tb[slot][q, jnp.minimum(at, 7)]
                dn[pl.ds(pl.multiple_of(i * BLK, BLK), BLK), q * BLK:(q + 1) * BLK] = jnp.where(
                    at < 8, tile, jnp.zeros_like(tile)
                )
            return 0

        lax.fori_loop(0, 16, block, 0)

    def c1_copy(mr):
        return pltpu.make_async_remote_copy(
            src_ref=c1s.at[mr], dst_ref=c1r.at[mr], send_sem=c1_send.at[mr],
            recv_sem=c1_recv.at[mr], device_id=core, device_id_type=MESH,
        )

    def rs_copy(mr, ch):
        at, n = CHUNKS[ch]
        return pltpu.make_async_remote_copy(
            src_ref=rss.at[mr, pl.ds(at, n)], dst_ref=rs.at[back(mr), pl.ds(at, n)],
            send_sem=rs_send.at[ch, mr], recv_sem=rs_recv.at[ch, back(mr)],
            device_id=chip(mr), device_id_type=MESH,
        )

    def ag_copy(mr, ch):
        rows = pl.ds(PAD + 128 * ch, 128)
        return pltpu.make_async_remote_copy(
            src_ref=re.at[0, 0, rows], dst_ref=re.at[0, back(mr), rows],
            send_sem=ag_send.at[ch, mr], recv_sem=ag_recv.at[ch, back(mr)],
            device_id=chip(mr), device_id_type=MESH,
        )

    def c2_copy(ch):
        rows = pl.ds(PAD + 128 * ch, 128)
        return pltpu.make_async_remote_copy(
            src_ref=re.at[0, :, rows], dst_ref=re.at[1, :, rows], send_sem=c2_send.at[ch],
            recv_sem=c2_recv.at[ch], device_id=core, device_id_type=MESH,
        )

    def each(first, last, body):
        def step(i, _):
            body(i)
            return 0

        lax.fori_loop(first, last, step, 0)

    out_ref[...] = vol_ref[...]
    xe[0:PAD] = jnp.ones((PAD, PIXELS), jnp.bfloat16)
    xe[PAD:] = vol_ref[...].astype(jnp.bfloat16)
    re[:, :, 0:PAD] = jnp.ones((2, CHIPS, PAD, BLK), jnp.bfloat16)
    assemble(0)

    for step in range(STEPS):
        dn = dense.at[step % 2]

        def forward(i):
            mr = CHIPS - 1 - i
            rows = dn[pl.ds(pl.multiple_of(mr * 256, 256), 256), :]
            y = lax.dot_general(
                xe[...], rows, (((1,), (1,)), ((), ())), preferred_element_type=jnp.float32
            )
            w = y[0:PAD]
            diff = y[PAD:] - y[0:1]
            mine[mr, 0:PAD] = w[:, :BLK]
            mine[mr, PAD:] = diff[:, :BLK]
            c1s[mr, 0:PAD] = split3(w[:, BLK:])
            c1s[mr, PAD:] = diff[:, BLK:].astype(jnp.bfloat16)
            c1_copy(mr).start()

        each(0, CHIPS, forward)
        if step + 2 < STEPS:
            pm_copy(step + 2).start()

        def chip_sum0(i):
            mr = CHIPS - 1 - i
            c1_copy(mr).wait_recv()
            w = mine[mr, 0:PAD] + jnp.sum(c1r[mr, 0:PAD].astype(jnp.float32), axis=0, keepdims=True)
            rss[mr, 0:PAD] = split3(w)
            n = CHUNKS[0][1]
            rss[mr, PAD:n] = (mine[mr, PAD:n] + c1r[mr, PAD:n].astype(jnp.float32)).astype(jnp.bfloat16)
            rs_copy(mr, 0).start()

        def chip_sum1(i):
            mr = CHIPS - 1 - i
            at = CHUNKS[1][0]
            rss[mr, at:] = (mine[mr, at:] + c1r[mr, at:].astype(jnp.float32)).astype(jnp.bfloat16)
            rs_copy(mr, 1).start()

        each(0, CHIPS - 1, chip_sum0)
        each(0, CHIPS - 1, chip_sum1)
        c1_copy(0).wait_recv()
        loc[0:PAD] = mine[0, 0:PAD] + jnp.sum(c1r[0, 0:PAD].astype(jnp.float32), axis=0, keepdims=True)
        loc[PAD:] = mine[0, PAD:] + c1r[0, PAD:].astype(jnp.float32)
        if step:
            pm_copy(step).wait_recv()

        for ch in range(2):
            each(1, CHIPS, lambda mr: rs_copy(mr, ch).wait_recv())
            at, n = CHUNKS[ch]
            if ch == 0:
                weights = rs[1, 0:PAD].astype(jnp.float32)
                for mr in range(2, CHIPS):
                    weights += rs[mr, 0:PAD].astype(jnp.float32)
                wtot[...] = loc[0:PAD] + jnp.sum(weights, axis=0, keepdims=True)
            first = max(at, PAD)
            total = loc[first:at + n]
            for mr in range(1, CHIPS):
                total += rs[mr, first:at + n].astype(jnp.float32)
            if step:
                measured = pm[step, 128 * ch:128 * ch + 128]
            else:
                measured = proj_ref[pl.ds(pl.multiple_of(c * COLS + 128 * ch, 128), 128), :]
            re[0, 0, first:at + n] = ((measured - 1.0) - total / wtot[0:1]).astype(jnp.bfloat16)
            each(1, CHIPS, lambda i: ag_copy(CHIPS - i, ch).start())

        for ch in range(2):
            each(1, CHIPS, lambda mr: ag_copy(mr, ch).wait_recv())
            c2_copy(ch).start()
        each(0, CHIPS, lambda mr: c1_copy(mr).wait_send())
        for ch in range(2):
            each(1, CHIPS, lambda mr: rs_copy(mr, ch).wait_send())
            each(1, CHIPS, lambda mr: ag_copy(mr, ch).wait_send())
        for ch in range(2):
            c2_copy(ch).wait()

        def backward(n):
            cols = pl.ds(pl.multiple_of(n * 256, 256), 256)
            acc = jnp.zeros((ROWS, 256), jnp.float32)
            for mr in range(CHIPS):
                lhs = jnp.concatenate([re[0, mr], re[1, mr]], axis=1)
                acc += jnp.dot(
                    lhs, dn[mr * 256:(mr + 1) * 256, cols], preferred_element_type=jnp.float32
                )
            new = out_ref[:, cols] + 0.9 * acc[PAD:] / acc[0:1]
            out_ref[:, cols] = new
            xe[PAD:, cols] = new.astype(jnp.bfloat16)

        each(0, 4, backward)
        if step == 0:
            tile_point(1)
        if step == 1:
            tile_point(3)
        if step == 2:
            tile_point(4)
        if step + 1 < STEPS:
            assemble(step + 1)
        if step == 0:
            tile_point(2)

    tile_drain()
    for slot in range(1, STEPS):
        inv_copy_to(slot).wait_send()
        pm_copy(slot).wait_send()


def per_device(start_volume, tiles, pattern, projections):
    entry = jnp.arange(8, dtype=jnp.int32)[None, :, None]
    name = jnp.arange(BLK, dtype=jnp.int32)[None, None, :]
    inverse = jnp.min(jnp.where(pattern[0][:, :, None] == name, entry, 8), axis=1)
    vmem = pl.BlockSpec(memory_space=pltpu.VMEM)
    bf16, f32, i32 = jnp.bfloat16, jnp.float32, jnp.int32
    dma = pltpu.SemaphoreType.DMA
    out = pl.pallas_call(
        kernel,
        out_shape=jax.ShapeDtypeStruct((COLS, PIXELS), f32),
        in_specs=[
            vmem, pl.BlockSpec(memory_space=pl.ANY), vmem,
            pl.BlockSpec(memory_space=pltpu.SMEM), vmem,
        ],
        out_specs=vmem,
        scratch_shapes=[
            [pltpu.VMEM((8, 8, BLK, BLK), bf16)] * STEPS,
            pltpu.VMEM((STEPS, 8, BLK), i32),
            pltpu.SMEM((STEPS, 8, BLK), i32),
            pltpu.VMEM((STEPS, COLS, BLK), f32),
            pltpu.VMEM((2, RAYS, PIXELS), bf16),
            pltpu.VMEM((ROWS, PIXELS), bf16),
            pltpu.VMEM((CHIPS, ROWS, BLK), f32),
            pltpu.VMEM((CHIPS, ROWS, BLK), bf16),
            pltpu.VMEM((CHIPS, ROWS, BLK), bf16),
            pltpu.VMEM((CHIPS, ROWS, BLK), bf16),
            pltpu.VMEM((CHIPS, ROWS, BLK), bf16),
            pltpu.VMEM((ROWS, BLK), f32),
            pltpu.VMEM((PAD, BLK), f32),
            pltpu.VMEM((2, CHIPS, ROWS, BLK), bf16),
            dma, dma((STEPS,)), dma((STEPS,)), dma, dma((STEPS,)), dma((STEPS,)),
            dma((15,)), dma((STEPS, 2)),
            dma((CHIPS,)), dma((CHIPS,)), dma((2, CHIPS)), dma((2, CHIPS)),
            dma((2, CHIPS)), dma((2, CHIPS)), dma((2,)), dma((2,)),
        ],
        compiler_params=pltpu.CompilerParams(
            collective_id=0, has_side_effects=True, vmem_limit_bytes=56 * 2**20
        ),
        cost_estimate=pl.CostEstimate(
            flops=STEPS * 4 * RAYS * PIXELS * COLS, bytes_accessed=6 * 2**20, transcendentals=0
        ),
        name="sweep",
    )(start_volume.T, tiles[0], inverse, inverse, projections[0].T)
    return out.T


def solution(mesh):
    in_specs = (
        P("tile", "subset"),
        P("subset", "tile", None, None, None),
        P("subset", "tile", None),
        P("subset", "tile", None),
    )
    return jax.shard_map(
        per_device, mesh=mesh, in_specs=in_specs, out_specs=P("tile", "subset"), check_vma=False
    )
```

```python
import jax
import jax.numpy as jnp
from jax import lax
from jax.experimental import pallas as pl
from jax.experimental.pallas import tpu as pltpu
from jax.sharding import PartitionSpec as P

MESH = pl.DeviceIdType.MESH
BLK = 128
STEPS = 8
CHIPS = 8
EARLY = 6
COLS = 256
PAD = 16
ROWS = COLS + PAD
PIXELS = 1024
RAYS = 2048
HALF = COLS // 2
LEAD = (PAD, 0)
SIZE = (PAD + HALF, HALF)


def split3(w):
    row = lax.broadcasted_iota(jnp.int32, w.shape, 0)
    hi = w.astype(jnp.bfloat16).astype(jnp.float32)
    rest = w - hi
    mid = rest.astype(jnp.bfloat16).astype(jnp.float32)
    low = rest - mid
    out = jnp.where(row == 0, hi, jnp.where(row == 1, mid, jnp.where(row == 2, low, 0.0)))
    return out.astype(jnp.bfloat16)


def kernel(
    vol_ref, tile_ref, inv_ref, inv0_ref, proj_ref, out_ref,
    tb, inv_v, inv_s, pm, dense, xe, wray, wtot, wpix, mine, c1s, c1r, rss, rsx, loc, re,
    tile_sem, inv_send, inv_recv, inv_copy, pm_send, pm_recv, t_send, t_recv,
    c1_send, c1_recv, rs_send, rs_recv, ag_send, ag_recv, c2_send, c2_recv,
):
    c = lax.axis_index("subset")
    t = lax.axis_index("tile")
    z, h = c // 2, c % 2
    x, l, k = t // 4, (t // 2) % 2, t % 2

    def chip(dx, dl):
        return (c, (((x + dx) % 4) * 2 + (l + dl) % 2) * 2 + k)

    core = (c, t + 1 - 2 * k)

    def group(d):
        return ((c + d) % STEPS, t)

    z_dev = {-1: (((z + 3) % 4) * 2 + h, t), 1: (((z + 1) % 4) * 2 + h, t)}
    y_dev = (z * 2 + 1 - h, t)

    def remote(src, dst, send, recv, device):
        return pltpu.make_async_remote_copy(
            src_ref=src, dst_ref=dst, send_sem=send, recv_sem=recv, device_id=device,
            device_id_type=MESH,
        )

    FAR = ((2, 1), (2, 0), (1, 1), (3, 1), (1, 0), (3, 0), (0, 1))

    own = pltpu.make_async_copy(tile_ref, tb[0], tile_sem)
    own.start()

    barrier = pltpu.get_barrier_semaphore()
    partners = [chip(dx, dl) for dx, dl in FAR] + [core]
    partners += [group(d) for d in range(1, STEPS)]
    for device in partners:
        pl.semaphore_signal(barrier, inc=1, device_id=device, device_id_type=MESH)
    pl.semaphore_wait(barrier, len(partners))
    own.wait()

    def piece(slot, p):
        return tb[slot].at[pl.ds(4 * p, 4)]

    def tile_copy(idx, src, p, dst, device):
        return remote(piece(src, p), piece(dst, p), t_send.at[idx], t_recv.at[dst, p], device)

    flows = (
        (
            (("-", 0, 0, 2), ("+", 0, 0, 6), ("y", 0, 1, 7)),
            (("-", 0, 1, 2), ("+", 6, 0, 4), ("y", 2, 0, 1)),
            (("-", 1, 1, 3), ("+", 0, 1, 6), ("y", 0, 0, 7)),
            (("-", 1, 0, 3), ("+", 1, 0, 7)),
            (("-", 2, 1, 4), ("+", 7, 0, 5)),
            (("-", 3, 1, 5), ("+", 1, 1, 7)),
        ),
        (
            (("-", 0, 0, 2), ("+", 0, 0, 6), ("y", 0, 1, 1)),
            (("-", 7, 1, 1), ("+", 7, 1, 5), ("y", 0, 0, 1)),
            (("-", 0, 1, 2), ("+", 5, 1, 3)),
            (("-", 1, 0, 3), ("+", 0, 1, 6)),
            (("-", 2, 0, 4), ("+", 6, 1, 4)),
            (("+", 7, 0, 5),),
        ),
    )
    events = [("send", 0), ("send", 1), ("make", 1), ("send", 2)]
    for slot in range(2, STEPS):
        if slot + 1 < len(flows[0]):
            events.append(("send", slot + 1))
        events.append(("make", slot))
    waits = ({}, {})
    for row in range(2):
        seen = set()
        for kind, at in events:
            if kind == "send":
                reads = sorted({(src, p) for _, src, p, _ in flows[row][at] if src})
            else:
                reads = [(at, 0), (at, 1)]
            waits[row][kind, at] = [r for r in reads if r not in seen]
            seen.update(reads)

    def tile_arrived(row, kind, at):
        for slot, p in waits[row][kind, at]:
            tile_copy(0, slot, p, slot, y_dev).wait_recv()

    def flow_copies(row, point):
        for i, (way, src, p, dst) in enumerate(flows[row][point]):
            device = y_dev if way == "y" else z_dev[-1 if way == "-" else 1]
            yield tile_copy(3 * point + i, src, p, dst, device)

    def tile_point(point):
        for row in range(2):
            @pl.when(h == row)
            def _():
                tile_arrived(row, "send", point)
                for copy in flow_copies(row, point):
                    copy.start()

    def tile_drain():
        for row in range(2):
            @pl.when(h == row)
            def _():
                for point in range(len(flows[row])):
                    for copy in flow_copies(row, point):
                        copy.wait_send()

    def tile_wait(slot):
        for row in range(2):
            @pl.when(h == row)
            def _():
                tile_arrived(row, "make", slot)

    def proj_rows(d):
        return pl.ds(pl.multiple_of(((c + d) % STEPS) * COLS, COLS), COLS)

    def pm_copy(slot):
        d = STEPS - slot
        return remote(
            proj_ref.at[proj_rows(d)], pm.at[slot], pm_send.at[slot], pm_recv.at[slot], group(d)
        )

    def inv_copy_to(slot):
        return remote(
            inv_ref, inv_v.at[slot], inv_send.at[slot], inv_recv.at[slot], group(STEPS - slot)
        )

    for slot in range(1, STEPS):
        inv_copy_to(slot).start()
    pm_copy(1).start()
    tile_point(0)

    def assemble(slot):
        dn = dense.at[slot % 3]
        if slot:
            inv_copy_to(slot).wait_recv()
            local = pltpu.make_async_copy(inv_v.at[slot], inv_s.at[slot], inv_copy)
            local.start()
            local.wait()
            tile_wait(slot)

        def block(i, _):
            mr, j = i // 2, i % 2
            b = (((x + mr % 4) % 4) * 2 + (l + mr // 4) % 2) * 2 + (k + j) % 2
            for q in range(8):
                at = inv_s[slot, q, b] if slot else inv0_ref[q, b]
                tile = tb[slot][q, jnp.minimum(at, 7)]
                dn[pl.ds(pl.multiple_of(i * BLK, BLK), BLK), q * BLK:(q + 1) * BLK] = jnp.where(
                    at < 8, tile, jnp.zeros_like(tile)
                )
            return 0

        lax.fori_loop(0, 16, block, 0)

    def c1_copy(hf, dl):
        part = pl.ds(4 * dl, 4)
        return remote(
            c1s[hf].at[part], c1r[hf].at[part], c1_send.at[hf, dl], c1_recv.at[hf, dl], core
        )

    def rs_copy(hf, dx, dl):
        out, into = 4 * dl + dx, 4 * dl + (4 - dx) % 4
        return remote(
            rss[hf].at[out], rsx[hf].at[into], rs_send.at[hf, out], rs_recv.at[hf, into],
            chip(dx, dl),
        )

    def ag_copy(hf, dx, dl):
        rows = pl.ds(LEAD[hf], HALF)
        out, into = 4 * dl + dx, 4 * dl + (4 - dx) % 4
        return remote(
            re[hf].at[0, 0, rows], re[hf].at[0, into, rows], ag_send.at[hf, out],
            ag_recv.at[hf, into], chip(dx, dl),
        )

    def c2_copy(hf):
        rows = pl.ds(LEAD[hf], HALF)
        return remote(
            re[hf].at[0, :, rows], re[hf].at[1, :, rows], c2_send.at[hf], c2_recv.at[hf], core
        )

    f32, bf16 = jnp.float32, jnp.bfloat16

    def forward(hf, dn):
        lhs = xe[0:SIZE[0]] if hf == 0 else xe[SIZE[0]:]
        for dl in (1, 0):
            for mr in range(4 * dl, 4 * dl + 4):
                y = lax.dot_general(
                    lhs, dn[mr * 256:(mr + 1) * 256, :], (((1,), (1,)), ((), ())),
                    preferred_element_type=f32,
                )
                if hf == 0:
                    w = y[0:PAD]
                    wray[mr] = w
                    mine[hf][mr, 0:PAD] = w[:, :BLK]
                    c1s[hf][mr, 0:PAD] = split3(w[:, BLK:])
                diff = y[LEAD[hf]:] - wray[mr, 0:1]
                mine[hf][mr, LEAD[hf]:] = diff[:, :BLK]
                c1s[hf][mr, LEAD[hf]:] = diff[:, BLK:].astype(bf16)
            c1_copy(hf, dl).start()

    def backward(hf, dn):
        lead = LEAD[hf]
        at = SIZE[0] if hf else PAD
        for n in range(4):
            cols = slice(n * 256, (n + 1) * 256)
            acc = jnp.zeros((SIZE[hf], 256), f32)
            for mr in range(CHIPS):
                lhs = jnp.concatenate([re[hf][0, mr], re[hf][1, mr]], axis=1)
                acc += jnp.dot(lhs, dn[mr * 256:(mr + 1) * 256, cols], preferred_element_type=f32)
            if hf == 0:
                wpix[:, cols] = acc[0:8]
            mine_rows = slice(hf * HALF, (hf + 1) * HALF)
            new = out_ref[mine_rows, cols] + 0.9 * acc[lead:] / wpix[0:1, cols]
            out_ref[mine_rows, cols] = new
            xe[at:at + HALF, cols] = new.astype(bf16)

    def stage_b(hf, dn):
        c2_copy(hf).wait()
        backward(hf, dn)

    def rows_sum(v):
        return jnp.sum(v.astype(f32), axis=0, keepdims=True)

    def stage_s(hf):
        lead = LEAD[hf]
        c1_copy(hf, 1).wait_recv()
        c1_copy(hf, 0).wait_recv()
        for dx, dl in FAR + ((0, 0),):
            mr = 4 * dl + dx
            data = mine[hf][mr, lead:] + c1r[hf][mr, lead:].astype(f32)
            if mr:
                rss[hf][mr, lead:] = data.astype(bf16)
            else:
                loc[hf][lead:] = data
            if hf == 0:
                w = mine[hf][mr, 0:PAD] + rows_sum(c1r[hf][mr, 0:PAD])
                if mr:
                    rss[hf][mr, 0:PAD] = split3(w)
                else:
                    loc[hf][0:PAD] = w
            if mr:
                rs_copy(hf, dx, dl).start()

    def stage_r(hf, step):
        lead = LEAD[hf]
        total = loc[hf][lead:]
        for dx, dl in reversed(FAR):
            into = 4 * dl + (4 - dx) % 4
            rs_copy(hf, dx, dl).wait_recv()
            total += rsx[hf][into, lead:].astype(f32)
        if hf == 0:
            w = rsx[hf][1, 0:PAD].astype(f32)
            for mr in range(2, CHIPS):
                w += rsx[hf][mr, 0:PAD].astype(f32)
            wtot[...] = loc[hf][0:PAD] + jnp.sum(w, axis=0, keepdims=True)
        measured = pm[step, hf * HALF:(hf + 1) * HALF]
        re[hf][0, 0, lead:] = ((measured - 1.0) - total / wtot[0:1]).astype(bf16)
        for dx, dl in FAR:
            ag_copy(hf, dx, dl).start()

    def stage_g(hf):
        for dx, dl in FAR:
            ag_copy(hf, dx, dl).wait_recv()
        c2_copy(hf).start()
        for dl in range(2):
            c1_copy(hf, dl).wait_send()
        for dx, dl in FAR:
            rs_copy(hf, dx, dl).wait_send()
            ag_copy(hf, dx, dl).wait_send()

    out_ref[...] = vol_ref[...]
    xe[0:PAD] = jnp.ones((PAD, PIXELS), bf16)
    xe[PAD:] = vol_ref[...].astype(bf16)
    re[0][:, :, 0:PAD] = jnp.ones((2, CHIPS, PAD, BLK), bf16)
    pm[0] = proj_ref[proj_rows(0)]
    assemble(0)

    forward(0, dense.at[0])
    pm_copy(2).start()
    stage_s(0)
    forward(1, dense.at[0])
    stage_s(1)
    stage_r(0, 0)
    stage_g(0)
    tile_point(1)
    assemble(1)
    tile_point(2)

    def period(step, _):
        dn, before = dense.at[step % 3], dense.at[(step + 2) % 3]
        stage_b(0, before)
        forward(0, dn)
        stage_r(1, step - 1)
        stage_s(0)
        for slot in range(EARLY, STEPS):
            @pl.when(step == slot - 1)
            def _():
                assemble(slot)
        stage_g(1)
        stage_b(1, before)
        forward(1, dn)
        pm_copy(step).wait_recv()
        stage_r(0, step)
        stage_s(1)
        stage_g(0)
        @pl.when(step + 2 < STEPS)
        def _():
            pm_copy(step + 2).start()
        for slot in range(2, EARLY):
            @pl.when(step == slot - 1)
            def _():
                if slot < 5:
                    tile_point(slot + 1)
                assemble(slot)
        return 0

    lax.fori_loop(1, STEPS, period, 0)

    last = dense.at[(STEPS - 1) % 3]
    stage_b(0, last)
    stage_r(1, STEPS - 1)
    stage_g(1)
    stage_b(1, last)

    tile_drain()
    for slot in range(1, STEPS):
        inv_copy_to(slot).wait_send()
        pm_copy(slot).wait_send()


def per_device(start_volume, tiles, pattern, projections):
    entry = jnp.arange(8, dtype=jnp.int32)[None, :, None]
    name = jnp.arange(BLK, dtype=jnp.int32)[None, None, :]
    inverse = jnp.min(jnp.where(pattern[0][:, :, None] == name, entry, 8), axis=1)
    vmem = pl.BlockSpec(memory_space=pltpu.VMEM)
    bf16, f32, i32 = jnp.bfloat16, jnp.float32, jnp.int32
    dma = pltpu.SemaphoreType.DMA
    out = pl.pallas_call(
        kernel,
        out_shape=jax.ShapeDtypeStruct((COLS, PIXELS), f32),
        in_specs=[
            vmem, pl.BlockSpec(memory_space=pl.ANY), vmem,
            pl.BlockSpec(memory_space=pltpu.SMEM), vmem,
        ],
        out_specs=vmem,
        scratch_shapes=[
            [pltpu.VMEM((8, 8, BLK, BLK), bf16)] * STEPS,
            pltpu.VMEM((STEPS, 8, BLK), i32),
            pltpu.SMEM((STEPS, 8, BLK), i32),
            pltpu.VMEM((STEPS, COLS, BLK), f32),
            pltpu.VMEM((3, RAYS, PIXELS), bf16),
            pltpu.VMEM((ROWS, PIXELS), bf16),
            pltpu.VMEM((CHIPS, PAD, 2 * BLK), f32),
            pltpu.VMEM((PAD, BLK), f32),
            pltpu.VMEM((8, PIXELS), f32),
            [pltpu.VMEM((CHIPS, n, BLK), f32) for n in SIZE],
            [pltpu.VMEM((CHIPS, n, BLK), bf16) for n in SIZE],
            [pltpu.VMEM((CHIPS, n, BLK), bf16) for n in SIZE],
            [pltpu.VMEM((CHIPS, n, BLK), bf16) for n in SIZE],
            [pltpu.VMEM((CHIPS, n, BLK), bf16) for n in SIZE],
            [pltpu.VMEM((n, BLK), f32) for n in SIZE],
            [pltpu.VMEM((2, CHIPS, n, BLK), bf16) for n in SIZE],
            dma, dma((STEPS,)), dma((STEPS,)), dma, dma((STEPS,)), dma((STEPS,)),
            dma((18,)), dma((STEPS, 2)),
            dma((2, 2)), dma((2, 2)), dma((2, CHIPS)), dma((2, CHIPS)),
            dma((2, CHIPS)), dma((2, CHIPS)), dma((2,)), dma((2,)),
        ],
        compiler_params=pltpu.CompilerParams(
            collective_id=0, has_side_effects=True, vmem_limit_bytes=56 * 2**20
        ),
        cost_estimate=pl.CostEstimate(
            flops=STEPS * 4 * RAYS * PIXELS * COLS, bytes_accessed=6 * 2**20, transcendentals=0
        ),
        name="sweep",
    )(start_volume.T, tiles[0], inverse, inverse, projections[0].T)
    return out.T


def solution(mesh):
    in_specs = (
        P("tile", "subset"),
        P("subset", "tile", None, None, None),
        P("subset", "tile", None),
        P("subset", "tile", None),
    )
    return jax.shard_map(
        per_device, mesh=mesh, in_specs=in_specs, out_specs=P("tile", "subset"), check_vma=False
    )
```

```python
import jax
import jax.numpy as jnp
from jax import lax
from jax.experimental import pallas as pl
from jax.experimental.pallas import tpu as pltpu
from jax.sharding import PartitionSpec as P

MESH = pl.DeviceIdType.MESH
BLK = 128
STEPS = 8
CHIPS = 8
EARLY = 4
COLS = 256
PAD = 16
ROWS = COLS + PAD
PIXELS = 1024
RAYS = 2048
HALF = COLS // 2
LEAD = (PAD, 0)
SIZE = (PAD + HALF, HALF)


def split3(w):
    row = lax.broadcasted_iota(jnp.int32, w.shape, 0)
    hi = w.astype(jnp.bfloat16).astype(jnp.float32)
    rest = w - hi
    mid = rest.astype(jnp.bfloat16).astype(jnp.float32)
    low = rest - mid
    out = jnp.where(row == 0, hi, jnp.where(row == 1, mid, jnp.where(row == 2, low, 0.0)))
    return out.astype(jnp.bfloat16)


def kernel(
    vol_ref, tile_ref, pat_ref, proj_ref, out_ref,
    tb, inv_v, inv_s, pm, dense, xe, wray, wtot, wpix, mine, c1s, c1r, rss, rsx, loc, re,
    tile_sem, inv_send, inv_recv, inv_copy, pm_send, pm_recv, t_send, t_recv,
    c1_send, c1_recv, rs_send, rs_recv, ag_send, ag_recv, c2_send, c2_recv,
):
    c = lax.axis_index("subset")
    t = lax.axis_index("tile")
    z, h = c // 2, c % 2
    x, l, k = t // 4, (t // 2) % 2, t % 2

    def chip(dx, dl):
        return (c, (((x + dx) % 4) * 2 + (l + dl) % 2) * 2 + k)

    core = (c, t + 1 - 2 * k)

    def group(d):
        return ((c + d) % STEPS, t)

    z_dev = {-1: (((z + 3) % 4) * 2 + h, t), 1: (((z + 1) % 4) * 2 + h, t)}
    y_dev = (z * 2 + 1 - h, t)

    def remote(src, dst, send, recv, device):
        return pltpu.make_async_remote_copy(
            src_ref=src, dst_ref=dst, send_sem=send, recv_sem=recv, device_id=device,
            device_id_type=MESH,
        )

    FAR = ((2, 1), (2, 0), (1, 1), (3, 1), (1, 0), (3, 0), (0, 1))

    own = pltpu.make_async_copy(tile_ref, tb[0], tile_sem)
    own.start()

    barrier = pltpu.get_barrier_semaphore()
    partners = [chip(dx, dl) for dx, dl in FAR] + [core]
    partners += [group(d) for d in range(1, STEPS)]
    for device in partners:
        pl.semaphore_signal(barrier, inc=1, device_id=device, device_id_type=MESH)
    pl.semaphore_wait(barrier, len(partners))
    own.wait()

    def piece(slot, q, n):
        return tb[slot].at[pl.ds(q, n)]

    def tile_copy(idx, src, q, n, dst, device):
        return remote(
            piece(src, q, n), piece(dst, q, n), t_send.at[idx], t_recv.at[dst, q // 2], device
        )

    flows = (
        (
            (("-", 0, 0, 2, 2), ("+", 0, 0, 4, 6), ("y", 0, 4, 2, 7)),
            (("-", 0, 2, 2, 2), ("y", 0, 6, 2, 7)),
            (("-", 0, 4, 4, 2), ("y", 2, 0, 2, 1)),
            (("y", 2, 2, 2, 1), ("+", 6, 0, 4, 4), ("-", 1, 4, 4, 3)),
            (("-", 1, 0, 4, 3), ("+", 0, 4, 4, 6), ("y", 0, 0, 4, 7)),
            (("-", 2, 4, 4, 4), ("+", 1, 0, 4, 7)),
            (("-", 3, 4, 4, 5), ("+", 7, 0, 4, 5)),
            (("+", 1, 4, 4, 7),),
        ),
        (
            (("-", 0, 0, 2, 2), ("+", 0, 0, 4, 6), ("y", 0, 4, 2, 1)),
            (("-", 0, 2, 2, 2), ("y", 0, 6, 2, 1)),
            (("-", 7, 4, 2, 1), ("+", 7, 4, 2, 5), ("y", 0, 0, 2, 1)),
            (("-", 7, 6, 2, 1), ("y", 0, 2, 2, 1), ("+", 7, 6, 2, 5), ("-", 0, 4, 4, 2)),
            (("-", 1, 0, 4, 3), ("+", 5, 4, 4, 3)),
            (("-", 2, 4, 4, 4), ("+", 6, 0, 4, 4)),
            (("+", 7, 0, 4, 5),),
            (("+", 0, 4, 4, 6),),
        ),
    )
    events = [("send", 0), ("send", 1), ("send", 2), ("send", 3), ("make", 1), ("send", 4)]
    for slot in range(2, STEPS):
        sends = [("send", slot + 3)] if slot + 3 < len(flows[0]) else []
        make = [("make", slot)]
        events += make + sends if slot >= EARLY else sends + make
    waits = ({}, {})
    for row in range(2):
        coming = []
        for other in range(2):
            for point in flows[other]:
                for way, _, q, n, dst in point:
                    if (way == "y") == (other != row):
                        coming.append((dst, q, n))
        for kind, at in events:
            if kind == "send":
                reads = [(src, q, n) for _, src, q, n, _ in flows[row][at]]
            else:
                reads = [(at, 0, 8)]
            waits[row][kind, at] = []
            for piece_in in tuple(coming):
                slot, q, n = piece_in
                if any(slot == s and q < p + m and p < q + n for s, p, m in reads):
                    waits[row][kind, at].append(piece_in)
                    coming.remove(piece_in)

    def tile_arrived(row, kind, at):
        for slot, q, n in waits[row][kind, at]:
            tile_copy(0, slot, q, n, slot, y_dev).wait_recv()

    def flow_copies(row, point):
        for i, (way, src, q, n, dst) in enumerate(flows[row][point]):
            device = y_dev if way == "y" else z_dev[-1 if way == "-" else 1]
            yield tile_copy(4 * point + i, src, q, n, dst, device)

    def tile_point(point):
        for row in range(2):
            if flows[row][point]:
                @pl.when(h == row)
                def _():
                    tile_arrived(row, "send", point)
                    for copy in flow_copies(row, point):
                        copy.start()

    def tile_drain():
        for row in range(2):
            @pl.when(h == row)
            def _():
                for point in range(len(flows[row])):
                    for copy in flow_copies(row, point):
                        copy.wait_send()

    def tile_wait(slot):
        for row in range(2):
            @pl.when(h == row)
            def _():
                tile_arrived(row, "make", slot)

    def proj_cols(d):
        return slice(None), pl.ds(pl.multiple_of(((c + d) % STEPS) * COLS, COLS), COLS)

    def pm_copy(slot):
        d = STEPS - slot
        return remote(
            proj_ref.at[proj_cols(d)], pm.at[slot], pm_send.at[slot], pm_recv.at[slot], group(d)
        )

    def inv_copy_to(slot):
        return remote(
            inv_v.at[0], inv_v.at[slot], inv_send.at[slot], inv_recv.at[slot], group(STEPS - slot)
        )

    tile_point(0)
    name = lax.broadcasted_iota(jnp.int32, (8, BLK), 1)
    inverse = jnp.full((8, BLK), 8, jnp.int32)
    for entry in range(8):
        inverse = jnp.where(pat_ref[:, entry:entry + 1] == name, entry, inverse)
    inv_v[0] = inverse
    for slot in range(1, STEPS):
        inv_copy_to(slot).start()
    pm_copy(1).start()

    def assemble(slot):
        dn = dense.at[slot % 3]
        if slot:
            inv_copy_to(slot).wait_recv()
        local = pltpu.make_async_copy(inv_v.at[slot], inv_s.at[slot], inv_copy)
        local.start()
        local.wait()
        if slot:
            tile_wait(slot)

        def block(i, _):
            mr, j = i // 2, i % 2
            b = (((x + mr % 4) % 4) * 2 + (l + mr // 4) % 2) * 2 + (k + j) % 2
            for q in range(8):
                at = inv_s[slot, q, b]
                tile = tb[slot][q, jnp.minimum(at, 7)]
                dn[pl.ds(pl.multiple_of(i * BLK, BLK), BLK), q * BLK:(q + 1) * BLK] = jnp.where(
                    at < 8, tile, jnp.zeros_like(tile)
                )
            return 0

        lax.fori_loop(0, 16, block, 0)

    def c1_copy(hf, dl):
        part = pl.ds(4 * dl, 4)
        return remote(
            c1s[hf].at[part], c1r[hf].at[part], c1_send.at[hf, dl], c1_recv.at[hf, dl], core
        )

    def rs_copy(hf, dx, dl):
        out, into = 4 * dl + dx, 4 * dl + (4 - dx) % 4
        return remote(
            rss[hf].at[out], rsx[hf].at[into], rs_send.at[hf, out], rs_recv.at[hf, into],
            chip(dx, dl),
        )

    def ag_copy(hf, dx, dl):
        rows = pl.ds(LEAD[hf], HALF)
        out, into = 4 * dl + dx, 4 * dl + (4 - dx) % 4
        return remote(
            re[hf].at[0, 0, rows], re[hf].at[0, into, rows], ag_send.at[hf, out],
            ag_recv.at[hf, into], chip(dx, dl),
        )

    def c2_copy(hf):
        rows = pl.ds(LEAD[hf], HALF)
        return remote(
            re[hf].at[0, :, rows], re[hf].at[1, :, rows], c2_send.at[hf], c2_recv.at[hf], core
        )

    f32, bf16 = jnp.float32, jnp.bfloat16

    def forward(hf, dn):
        lhs = xe[0:SIZE[0]] if hf == 0 else xe[SIZE[0]:]
        for dl in (1, 0):
            for mr in range(4 * dl, 4 * dl + 4):
                y = lax.dot_general(
                    lhs, dn[mr * 256:(mr + 1) * 256, :], (((1,), (1,)), ((), ())),
                    preferred_element_type=f32,
                )
                if hf == 0:
                    w = y[0:PAD]
                    wray[mr] = w
                    mine[hf][mr, 0:PAD] = w[:, :BLK]
                    c1s[hf][mr, 0:PAD] = split3(w[:, BLK:])
                diff = y[LEAD[hf]:] - wray[mr, 0:1]
                mine[hf][mr, LEAD[hf]:] = diff[:, :BLK]
                c1s[hf][mr, LEAD[hf]:] = diff[:, BLK:].astype(bf16)
            c1_copy(hf, dl).start()

    def backward(hf, dn):
        lead = LEAD[hf]
        at = SIZE[0] if hf else PAD
        for n in range(4):
            cols = slice(n * 256, (n + 1) * 256)
            acc = jnp.zeros((SIZE[hf], 256), f32)
            for mr in range(CHIPS):
                lhs = jnp.concatenate([re[hf][0, mr], re[hf][1, mr]], axis=1)
                acc += jnp.dot(lhs, dn[mr * 256:(mr + 1) * 256, cols], preferred_element_type=f32)
            if hf == 0:
                wpix[:, cols] = acc[0:8]
            mine_rows = slice(hf * HALF, (hf + 1) * HALF)
            new = out_ref[mine_rows, cols] + 0.9 * acc[lead:] / wpix[0:1, cols]
            out_ref[mine_rows, cols] = new
            xe[at:at + HALF, cols] = new.astype(bf16)

    def stage_b(hf, dn):
        c2_copy(hf).wait()
        backward(hf, dn)

    def rows_sum(v):
        return jnp.sum(v.astype(f32), axis=0, keepdims=True)

    def stage_s(hf):
        lead = LEAD[hf]
        c1_copy(hf, 1).wait_recv()
        c1_copy(hf, 0).wait_recv()
        for dx, dl in FAR + ((0, 0),):
            mr = 4 * dl + dx
            data = mine[hf][mr, lead:] + c1r[hf][mr, lead:].astype(f32)
            if mr:
                rss[hf][mr, lead:] = data.astype(bf16)
            else:
                loc[hf][lead:] = data
            if hf == 0:
                w = mine[hf][mr, 0:PAD] + rows_sum(c1r[hf][mr, 0:PAD])
                if mr:
                    rss[hf][mr, 0:PAD] = split3(w)
                else:
                    loc[hf][0:PAD] = w
            if mr:
                rs_copy(hf, dx, dl).start()

    def stage_r(hf, step):
        lead = LEAD[hf]
        measured = pm[step, :, hf * HALF:(hf + 1) * HALF].T - 1.0
        total = loc[hf][lead:]
        for dx, dl in reversed(FAR):
            into = 4 * dl + (4 - dx) % 4
            rs_copy(hf, dx, dl).wait_recv()
            total += rsx[hf][into, lead:].astype(f32)
        if hf == 0:
            w = rsx[hf][1, 0:PAD].astype(f32)
            for mr in range(2, CHIPS):
                w += rsx[hf][mr, 0:PAD].astype(f32)
            wtot[...] = loc[hf][0:PAD] + jnp.sum(w, axis=0, keepdims=True)
        re[hf][0, 0, lead:] = (measured - total / wtot[0:1]).astype(bf16)
        for dx, dl in FAR:
            ag_copy(hf, dx, dl).start()

    def stage_g(hf):
        for dx, dl in FAR:
            ag_copy(hf, dx, dl).wait_recv()
        c2_copy(hf).start()
        for dl in range(2):
            c1_copy(hf, dl).wait_send()
        for dx, dl in FAR:
            rs_copy(hf, dx, dl).wait_send()
            ag_copy(hf, dx, dl).wait_send()

    for n in range(4):
        out_ref[:, n * 256:(n + 1) * 256] = vol_ref[n * 256:(n + 1) * 256, :].T
    xe[0:PAD] = jnp.ones((PAD, PIXELS), bf16)
    xe[PAD:] = out_ref[...].astype(bf16)
    re[0][:, :, 0:PAD] = jnp.ones((2, CHIPS, PAD, BLK), bf16)
    pm[0] = proj_ref[proj_cols(0)]
    assemble(0)

    forward(0, dense.at[0])
    pm_copy(2).start()
    stage_s(0)
    forward(1, dense.at[0])
    stage_s(1)
    tile_point(1)
    stage_r(0, 0)
    stage_g(0)
    tile_point(2)
    tile_point(3)
    assemble(1)
    tile_point(4)

    def period(step, _):
        dn, before = dense.at[step % 3], dense.at[(step + 2) % 3]
        stage_b(0, before)
        forward(0, dn)
        stage_r(1, step - 1)
        stage_s(0)
        for slot in range(EARLY, STEPS):
            @pl.when(step == slot - 1)
            def _():
                assemble(slot)
        stage_g(1)
        stage_b(1, before)
        forward(1, dn)
        pm_copy(step).wait_recv()
        stage_r(0, step)
        stage_s(1)
        stage_g(0)
        @pl.when(step + 2 < STEPS)
        def _():
            pm_copy(step + 2).start()
        for slot in range(2, STEPS):
            if slot < EARLY or slot + 3 < len(flows[0]):
                @pl.when(step == slot - 1)
                def _():
                    if slot + 3 < len(flows[0]):
                        tile_point(slot + 3)
                    if slot < EARLY:
                        assemble(slot)
        return 0

    lax.fori_loop(1, STEPS, period, 0)

    last = dense.at[(STEPS - 1) % 3]
    stage_b(0, last)
    stage_r(1, STEPS - 1)
    stage_g(1)
    stage_b(1, last)

    tile_drain()
    for slot in range(1, STEPS):
        inv_copy_to(slot).wait_send()
        pm_copy(slot).wait_send()


def per_device(start_volume, tiles, pattern, projections):
    vmem = pl.BlockSpec(memory_space=pltpu.VMEM)
    bf16, f32, i32 = jnp.bfloat16, jnp.float32, jnp.int32
    dma = pltpu.SemaphoreType.DMA
    out = pl.pallas_call(
        kernel,
        out_shape=jax.ShapeDtypeStruct((COLS, PIXELS), f32),
        in_specs=[
            vmem, pl.BlockSpec(memory_space=pl.ANY), vmem, vmem,
        ],
        out_specs=vmem,
        scratch_shapes=[
            [pltpu.VMEM((8, 8, BLK, BLK), bf16)] * STEPS,
            pltpu.VMEM((STEPS, 8, BLK), i32),
            pltpu.SMEM((STEPS, 8, BLK), i32),
            pltpu.VMEM((STEPS, BLK, COLS), f32),
            pltpu.VMEM((3, RAYS, PIXELS), bf16),
            pltpu.VMEM((ROWS, PIXELS), bf16),
            pltpu.VMEM((CHIPS, PAD, 2 * BLK), f32),
            pltpu.VMEM((PAD, BLK), f32),
            pltpu.VMEM((8, PIXELS), f32),
            [pltpu.VMEM((CHIPS, n, BLK), f32) for n in SIZE],
            [pltpu.VMEM((CHIPS, n, BLK), bf16) for n in SIZE],
            [pltpu.VMEM((CHIPS, n, BLK), bf16) for n in SIZE],
            [pltpu.VMEM((CHIPS, n, BLK), bf16) for n in SIZE],
            [pltpu.VMEM((CHIPS, n, BLK), bf16) for n in SIZE],
            [pltpu.VMEM((n, BLK), f32) for n in SIZE],
            [pltpu.VMEM((2, CHIPS, n, BLK), bf16) for n in SIZE],
            dma, dma((STEPS,)), dma((STEPS,)), dma, dma((STEPS,)), dma((STEPS,)),
            dma((32,)), dma((STEPS, 4)),
            dma((2, 2)), dma((2, 2)), dma((2, CHIPS)), dma((2, CHIPS)),
            dma((2, CHIPS)), dma((2, CHIPS)), dma((2,)), dma((2,)),
        ],
        compiler_params=pltpu.CompilerParams(
            collective_id=0, has_side_effects=True, vmem_limit_bytes=56 * 2**20
        ),
        cost_estimate=pl.CostEstimate(
            flops=STEPS * 4 * RAYS * PIXELS * COLS, bytes_accessed=6 * 2**20, transcendentals=0
        ),
        name="sweep",
    )(start_volume, tiles[0], pattern[0], projections[0])
    return out.T


def solution(mesh):
    in_specs = (
        P("tile", "subset"),
        P("subset", "tile", None, None, None),
        P("subset", "tile", None),
        P("subset", "tile", None),
    )
    return jax.shard_map(
        per_device, mesh=mesh, in_specs=in_specs, out_specs=P("tile", "subset"), check_vma=False
    )
```

```python
import jax
import jax.numpy as jnp
from jax import lax
from jax.experimental import pallas as pl
from jax.experimental.pallas import tpu as pltpu
from jax.sharding import PartitionSpec as P

MESH = pl.DeviceIdType.MESH
BLK = 128
STEPS = 8
CHIPS = 8
EARLY = 4
COLS = 256
PAD = 16
ROWS = COLS + PAD
PIXELS = 1024
RAYS = 2048
HALF = COLS // 2
LEAD = (PAD, 0)
SIZE = (PAD + HALF, HALF)


def split3(w):
    row = lax.broadcasted_iota(jnp.int32, w.shape, 0)
    hi = w.astype(jnp.bfloat16).astype(jnp.float32)
    rest = w - hi
    mid = rest.astype(jnp.bfloat16).astype(jnp.float32)
    low = rest - mid
    out = jnp.where(row == 0, hi, jnp.where(row == 1, mid, jnp.where(row == 2, low, 0.0)))
    return out.astype(jnp.bfloat16)


def kernel(
    vol_ref, tile_ref, pat_ref, proj_ref, out_ref,
    tb, inv_v, inv_s, pm, dense, xe, wray, wtot, wpix, mine, c1s, c1r, rss, rsx, loc, re,
    tile_sem, inv_send, inv_recv, inv_copy, pm_send, pm_recv, t_send, t_recv,
    c1_send, c1_recv, rs_send, rs_recv, ag_send, ag_recv, c2_send, c2_recv,
):
    c = lax.axis_index("subset")
    t = lax.axis_index("tile")
    z, h = c // 2, c % 2
    x, l, k = t // 4, (t // 2) % 2, t % 2

    def chip(dx, dl):
        return (c, (((x + dx) % 4) * 2 + (l + dl) % 2) * 2 + k)

    core = (c, t + 1 - 2 * k)

    def group(d):
        return ((c + d) % STEPS, t)

    z_dev = {-1: (((z + 3) % 4) * 2 + h, t), 1: (((z + 1) % 4) * 2 + h, t)}
    y_dev = (z * 2 + 1 - h, t)

    def remote(src, dst, send, recv, device):
        return pltpu.make_async_remote_copy(
            src_ref=src, dst_ref=dst, send_sem=send, recv_sem=recv, device_id=device,
            device_id_type=MESH,
        )

    FAR = ((2, 1), (2, 0), (1, 1), (3, 1), (1, 0), (3, 0), (0, 1))

    own = pltpu.make_async_copy(tile_ref, tb[0], tile_sem)
    own.start()

    barrier = pltpu.get_barrier_semaphore()
    partners = [chip(dx, dl) for dx, dl in FAR] + [core]
    partners += [group(d) for d in range(1, STEPS)]
    for device in partners:
        pl.semaphore_signal(barrier, inc=1, device_id=device, device_id_type=MESH)
    pl.semaphore_wait(barrier, len(partners))
    own.wait()

    def piece(slot, q, n):
        return tb[slot].at[pl.ds(q, n)]

    def tile_copy(idx, src, q, n, dst, device):
        return remote(
            piece(src, q, n), piece(dst, q, n), t_send.at[idx], t_recv.at[dst, q // 2], device
        )

    flows = (
        (
            (("-", 0, 0, 2, 2), ("+", 0, 0, 4, 6), ("y", 0, 4, 2, 7)),
            (("-", 0, 2, 2, 2), ("y", 0, 6, 2, 7)),
            (("-", 0, 4, 4, 2), ("y", 2, 0, 2, 1)),
            (("y", 2, 2, 2, 1), ("+", 6, 0, 4, 4), ("-", 1, 4, 4, 3)),
            (("-", 1, 0, 4, 3), ("+", 0, 4, 4, 6), ("y", 0, 0, 4, 7)),
            (("-", 2, 4, 4, 4), ("+", 1, 0, 4, 7)),
            (("-", 3, 4, 4, 5), ("+", 7, 0, 4, 5)),
            (("+", 1, 4, 4, 7),),
        ),
        (
            (("-", 0, 0, 2, 2), ("+", 0, 0, 4, 6), ("y", 0, 4, 2, 1)),
            (("-", 0, 2, 2, 2), ("y", 0, 6, 2, 1)),
            (("-", 7, 4, 2, 1), ("+", 7, 4, 2, 5), ("y", 0, 0, 2, 1)),
            (("-", 7, 6, 2, 1), ("y", 0, 2, 2, 1), ("+", 7, 6, 2, 5), ("-", 0, 4, 4, 2)),
            (("-", 1, 0, 4, 3), ("+", 5, 4, 4, 3)),
            (("-", 2, 4, 4, 4), ("+", 6, 0, 4, 4)),
            (("+", 7, 0, 4, 5),),
            (("+", 0, 4, 4, 6),),
        ),
    )
    events = [("send", 0), ("send", 1), ("send", 2), ("send", 3), ("make", 1), ("send", 4)]
    for slot in range(2, STEPS):
        sends = [("send", slot + 3)] if slot + 3 < len(flows[0]) else []
        make = [("make", slot)]
        events += make + sends if slot >= EARLY else sends + make
    waits = ({}, {})
    for row in range(2):
        coming = []
        for other in range(2):
            for point in flows[other]:
                for way, _, q, n, dst in point:
                    if (way == "y") == (other != row):
                        coming.append((dst, q, n))
        for kind, at in events:
            if kind == "send":
                reads = [(src, q, n) for _, src, q, n, _ in flows[row][at]]
            else:
                reads = [(at, 0, 8)]
            waits[row][kind, at] = []
            for piece_in in tuple(coming):
                slot, q, n = piece_in
                if any(slot == s and q < p + m and p < q + n for s, p, m in reads):
                    waits[row][kind, at].append(piece_in)
                    coming.remove(piece_in)

    def tile_arrived(row, kind, at):
        for slot, q, n in waits[row][kind, at]:
            tile_copy(0, slot, q, n, slot, y_dev).wait_recv()

    def flow_copies(row, point):
        for i, (way, src, q, n, dst) in enumerate(flows[row][point]):
            device = y_dev if way == "y" else z_dev[-1 if way == "-" else 1]
            yield tile_copy(4 * point + i, src, q, n, dst, device)

    def tile_point(point):
        for row in range(2):
            if flows[row][point]:
                @pl.when(h == row)
                def _():
                    tile_arrived(row, "send", point)
                    for copy in flow_copies(row, point):
                        copy.start()

    def tile_drain():
        for row in range(2):
            @pl.when(h == row)
            def _():
                for point in range(len(flows[row])):
                    for copy in flow_copies(row, point):
                        copy.wait_send()

    def tile_wait(slot):
        for row in range(2):
            @pl.when(h == row)
            def _():
                tile_arrived(row, "make", slot)

    def proj_cols(d):
        return slice(None), pl.ds(pl.multiple_of(((c + d) % STEPS) * COLS, COLS), COLS)

    def pm_copy(slot):
        d = STEPS - slot
        return remote(
            proj_ref.at[proj_cols(d)], pm.at[slot], pm_send.at[slot], pm_recv.at[slot], group(d)
        )

    def inv_copy_to(slot):
        return remote(
            inv_v.at[0], inv_v.at[slot], inv_send.at[slot], inv_recv.at[slot], group(STEPS - slot)
        )

    tile_point(0)
    name = lax.broadcasted_iota(jnp.int32, (8, BLK), 1)
    inverse = jnp.full((8, BLK), 8, jnp.int32)
    for entry in range(8):
        inverse = jnp.where(pat_ref[:, entry:entry + 1] == name, entry, inverse)
    inv_v[0] = inverse
    for slot in range(1, STEPS):
        inv_copy_to(slot).start()
    pm_copy(1).start()

    def assemble(slot):
        dn = dense.at[slot % 3]
        if slot:
            inv_copy_to(slot).wait_recv()
        local = pltpu.make_async_copy(inv_v.at[slot], inv_s.at[slot], inv_copy)
        local.start()
        local.wait()
        if slot:
            tile_wait(slot)

        def block(i, _):
            mr, j = i // 2, i % 2
            b = (((x + mr % 4) % 4) * 2 + (l + mr // 4) % 2) * 2 + (k + j) % 2
            for q in range(8):
                at = inv_s[slot, q, b]
                tile = tb[slot][q, jnp.minimum(at, 7)]
                dn[pl.ds(pl.multiple_of(i * BLK, BLK), BLK), q * BLK:(q + 1) * BLK] = jnp.where(
                    at < 8, tile, jnp.zeros_like(tile)
                )
            return 0

        lax.fori_loop(0, 16, block, 0)

    def c1_copy(hf, dl):
        part = pl.ds(4 * dl, 4)
        return remote(
            c1s[hf].at[part], c1r[hf].at[part], c1_send.at[hf, dl], c1_recv.at[hf, dl], core
        )

    def rs_copy(hf, dx, dl):
        out, into = 4 * dl + dx, 4 * dl + (4 - dx) % 4
        return remote(
            rss[hf].at[out], rsx[hf].at[into], rs_send.at[hf, out], rs_recv.at[hf, into],
            chip(dx, dl),
        )

    def ag_copy(hf, dx, dl):
        rows = pl.ds(LEAD[hf], HALF)
        out, into = 4 * dl + dx, 4 * dl + (4 - dx) % 4
        return remote(
            re[hf].at[0, 0, rows], re[hf].at[0, into, rows], ag_send.at[hf, out],
            ag_recv.at[hf, into], chip(dx, dl),
        )

    def c2_copy(hf):
        rows = pl.ds(LEAD[hf], HALF)
        return remote(
            re[hf].at[0, :, rows], re[hf].at[1, :, rows], c2_send.at[hf], c2_recv.at[hf], core
        )

    f32, bf16 = jnp.float32, jnp.bfloat16

    def forward(hf, dn):
        lhs = xe[0:SIZE[0]] if hf == 0 else xe[SIZE[0]:]
        for dl in (1, 0):
            for mr in range(4 * dl, 4 * dl + 4):
                y = lax.dot_general(
                    lhs, dn[mr * 256:(mr + 1) * 256, :], (((1,), (1,)), ((), ())),
                    preferred_element_type=f32,
                )
                if hf == 0:
                    w = y[0:PAD]
                    wray[mr] = w
                    mine[hf][mr, 0:PAD] = w[:, :BLK]
                    c1s[hf][mr, 0:PAD] = split3(w[:, BLK:])
                diff = y[LEAD[hf]:] - wray[mr, 0:1]
                mine[hf][mr, LEAD[hf]:] = diff[:, :BLK]
                c1s[hf][mr, LEAD[hf]:] = diff[:, BLK:].astype(bf16)
            c1_copy(hf, dl).start()

    def backward(hf, dn):
        lead = LEAD[hf]
        at = SIZE[0] if hf else PAD
        for n in range(4):
            cols = slice(n * 256, (n + 1) * 256)
            acc = jnp.zeros((SIZE[hf], 256), f32)
            for mr in range(CHIPS):
                lhs = jnp.concatenate([re[hf][0, mr], re[hf][1, mr]], axis=1)
                acc += jnp.dot(lhs, dn[mr * 256:(mr + 1) * 256, cols], preferred_element_type=f32)
            if hf == 0:
                wpix[:, cols] = acc[0:8]
            mine_rows = slice(hf * HALF, (hf + 1) * HALF)
            new = out_ref[mine_rows, cols] + 0.9 * acc[lead:] / wpix[0:1, cols]
            out_ref[mine_rows, cols] = new
            xe[at:at + HALF, cols] = new.astype(bf16)

    def stage_b(hf, dn):
        c2_copy(hf).wait()
        backward(hf, dn)

    def rows_sum(v):
        return jnp.sum(v.astype(f32), axis=0, keepdims=True)

    def stage_s(hf):
        lead = LEAD[hf]
        c1_copy(hf, 1).wait_recv()
        c1_copy(hf, 0).wait_recv()
        for dx, dl in FAR + ((0, 0),):
            mr = 4 * dl + dx
            data = mine[hf][mr, lead:] + c1r[hf][mr, lead:].astype(f32)
            if mr:
                rss[hf][mr, lead:] = data.astype(bf16)
            else:
                loc[hf][lead:] = data
            if hf == 0:
                w = mine[hf][mr, 0:PAD] + rows_sum(c1r[hf][mr, 0:PAD])
                if mr:
                    rss[hf][mr, 0:PAD] = split3(w)
                else:
                    loc[hf][0:PAD] = w
            if mr:
                rs_copy(hf, dx, dl).start()

    def stage_r(hf, step):
        lead = LEAD[hf]
        measured = pm[step, :, hf * HALF:(hf + 1) * HALF].T - 1.0
        total = loc[hf][lead:]
        for dx, dl in reversed(FAR):
            into = 4 * dl + (4 - dx) % 4
            rs_copy(hf, dx, dl).wait_recv()
            total += rsx[hf][into, lead:].astype(f32)
        if hf == 0:
            w = rsx[hf][1, 0:PAD].astype(f32)
            for mr in range(2, CHIPS):
                w += rsx[hf][mr, 0:PAD].astype(f32)
            wtot[...] = loc[hf][0:PAD] + jnp.sum(w, axis=0, keepdims=True)
        re[hf][0, 0, lead:] = (measured - total / wtot[0:1]).astype(bf16)
        for dx, dl in FAR:
            ag_copy(hf, dx, dl).start()

    def stage_g(hf):
        for dx, dl in FAR:
            ag_copy(hf, dx, dl).wait_recv()
        c2_copy(hf).start()
        for dl in range(2):
            c1_copy(hf, dl).wait_send()
        for dx, dl in FAR:
            rs_copy(hf, dx, dl).wait_send()
            ag_copy(hf, dx, dl).wait_send()

    for n in range(4):
        out_ref[:, n * 256:(n + 1) * 256] = vol_ref[n * 256:(n + 1) * 256, :].T
    xe[0:PAD] = jnp.ones((PAD, PIXELS), bf16)
    xe[PAD:] = out_ref[...].astype(bf16)
    re[0][:, :, 0:PAD] = jnp.ones((2, CHIPS, PAD, BLK), bf16)
    pm[0] = proj_ref[proj_cols(0)]
    assemble(0)

    forward(0, dense.at[0])
    pm_copy(2).start()
    stage_s(0)
    forward(1, dense.at[0])
    stage_s(1)
    tile_point(1)
    stage_r(0, 0)
    stage_g(0)
    tile_point(2)
    tile_point(3)
    assemble(1)
    tile_point(4)

    def period(step, _):
        dn, before = dense.at[step % 3], dense.at[(step + 2) % 3]
        stage_b(0, before)
        stage_r(1, step - 1)
        forward(0, dn)
        stage_s(0)
        for slot in range(EARLY, STEPS):
            @pl.when(step == slot - 1)
            def _():
                assemble(slot)
        stage_g(1)
        stage_b(1, before)
        pm_copy(step).wait_recv()
        stage_r(0, step)
        forward(1, dn)
        stage_s(1)
        stage_g(0)
        @pl.when(step + 2 < STEPS)
        def _():
            pm_copy(step + 2).start()
        for slot in range(2, STEPS):
            if slot < EARLY or slot + 3 < len(flows[0]):
                @pl.when(step == slot - 1)
                def _():
                    if slot + 3 < len(flows[0]):
                        tile_point(slot + 3)
                    if slot < EARLY:
                        assemble(slot)
        return 0

    lax.fori_loop(1, STEPS, period, 0)

    last = dense.at[(STEPS - 1) % 3]
    stage_b(0, last)
    stage_r(1, STEPS - 1)
    stage_g(1)
    stage_b(1, last)

    tile_drain()
    for slot in range(1, STEPS):
        inv_copy_to(slot).wait_send()
        pm_copy(slot).wait_send()


def per_device(start_volume, tiles, pattern, projections):
    vmem = pl.BlockSpec(memory_space=pltpu.VMEM)
    bf16, f32, i32 = jnp.bfloat16, jnp.float32, jnp.int32
    dma = pltpu.SemaphoreType.DMA
    out = pl.pallas_call(
        kernel,
        out_shape=jax.ShapeDtypeStruct((COLS, PIXELS), f32),
        in_specs=[
            vmem, pl.BlockSpec(memory_space=pl.ANY), vmem, vmem,
        ],
        out_specs=vmem,
        scratch_shapes=[
            [pltpu.VMEM((8, 8, BLK, BLK), bf16)] * STEPS,
            pltpu.VMEM((STEPS, 8, BLK), i32),
            pltpu.SMEM((STEPS, 8, BLK), i32),
            pltpu.VMEM((STEPS, BLK, COLS), f32),
            pltpu.VMEM((3, RAYS, PIXELS), bf16),
            pltpu.VMEM((ROWS, PIXELS), bf16),
            pltpu.VMEM((CHIPS, PAD, 2 * BLK), f32),
            pltpu.VMEM((PAD, BLK), f32),
            pltpu.VMEM((8, PIXELS), f32),
            [pltpu.VMEM((CHIPS, n, BLK), f32) for n in SIZE],
            [pltpu.VMEM((CHIPS, n, BLK), bf16) for n in SIZE],
            [pltpu.VMEM((CHIPS, n, BLK), bf16) for n in SIZE],
            [pltpu.VMEM((CHIPS, n, BLK), bf16) for n in SIZE],
            [pltpu.VMEM((CHIPS, n, BLK), bf16) for n in SIZE],
            [pltpu.VMEM((n, BLK), f32) for n in SIZE],
            [pltpu.VMEM((2, CHIPS, n, BLK), bf16) for n in SIZE],
            dma, dma((STEPS,)), dma((STEPS,)), dma, dma((STEPS,)), dma((STEPS,)),
            dma((32,)), dma((STEPS, 4)),
            dma((2, 2)), dma((2, 2)), dma((2, CHIPS)), dma((2, CHIPS)),
            dma((2, CHIPS)), dma((2, CHIPS)), dma((2,)), dma((2,)),
        ],
        compiler_params=pltpu.CompilerParams(
            collective_id=0, has_side_effects=True, vmem_limit_bytes=56 * 2**20
        ),
        cost_estimate=pl.CostEstimate(
            flops=STEPS * 4 * RAYS * PIXELS * COLS, bytes_accessed=6 * 2**20, transcendentals=0
        ),
        name="sweep",
    )(start_volume, tiles[0], pattern[0], projections[0])
    return out.T


def solution(mesh):
    in_specs = (
        P("tile", "subset"),
        P("subset", "tile", None, None, None),
        P("subset", "tile", None),
        P("subset", "tile", None),
    )
    return jax.shard_map(
        per_device, mesh=mesh, in_specs=in_specs, out_specs=P("tile", "subset"), check_vma=False
    )
```
